512 devices in a mesh: prow: 64 (over z, y), pcol: 8 (over x, core).
Axes of the slice: x: 4, y: 4, z: 16, core: 2. Of those that a mesh axis runs over, the one named last changes fastest.
Arguments:
- leaf_rhs: bfloat16 [1024, 64, 256], P(('prow', 'pcol')), may hold values from -6 to 6
- leaf_inverse: bfloat16 [1024, 256, 256], P(('prow', 'pcol')), as said below
- leaf_lower: bfloat16 [1024, 12, 256, 256], P(('prow', 'pcol')), may hold values from -0.02734375 to 0.02734375
- leaf_links: int32 [1024, 12], P(('prow', 'pcol')), may hold values from 0 to 63, as said below
- sep_rhs: bfloat16 [64, 64, 256], P('prow'), may hold values from -6 to 6
- sep_inverse: bfloat16 [64, 256, 256], P('prow'), as said below
Outputs:
- leaf_solution: bfloat16 [1024, 64, 256], P(('prow', 'pcol'))
- sep_solution: bfloat16 [64, 64, 256], P('prow')
The draws below stay inside these ranges and needn't reach their ends.
Inputs may be any that keep to these rules, and one draw needn't show every extreme that they name: `leaf_links`: leaf i lies on the device of block row p = i // 16; the 24 entries of the 2 leaves of one device (aligned blocks of 2 rows) are exactly the separators (p + d) mod 64 for d from -(12) to 10 and for d = 32, each once, in an order drawn for each device. `leaf_inverse`: lower triangular with a positive diagonal. `sep_inverse`: lower triangular with a positive diagonal.
All inputs are finite; a program needn't handle non-finite values.
Results may differ from the reference program's by a relative error of at most 0.0061.
Values may be sent and summed in bfloat16 or wider, within the bound.
No kernel may reach another device: no remote copies, remote signals or barrier semaphores. Data moves between devices by JAX's collectives and lax.ppermute only.
A program may use at most 64 MiB of HBM per device.

```python
import jax
import jax.numpy as jnp
from jax import lax

B = 256
R = 64
LEAF_DEV = 2
K = 12
NSEP = 64
NLEAF = 1024
N_PCOL = 8


def assemble(diagonal, off_part):
    order_size = diagonal.shape[-1]
    row_index = lax.broadcasted_iota(jnp.int32, (order_size, order_size), 0)
    col_index = lax.broadcasted_iota(jnp.int32, (order_size, order_size), 1)
    below = (col_index < row_index).astype(jnp.float32)
    on_diagonal = (col_index == row_index).astype(jnp.float32)
    return off_part * below * (0.7 / order_size ** 0.5) + diagonal[..., :, None] * on_diagonal


def draw_leaf_inverse(key, part):
    key = jax.random.fold_in(key, 11)
    key_diag, key_off = jax.random.split(key)
    diagonal = jnp.exp(jax.random.uniform(key_diag, (NLEAF, B), minval=-0.7, maxval=0.7))
    off_part = jax.random.normal(key_off, (NLEAF, B, B))
    return assemble(diagonal, off_part).astype(jnp.bfloat16)


def draw_sep_inverse(key, part):
    key = jax.random.fold_in(key, 23)
    key_diag, key_off = jax.random.split(key)
    diagonal = jnp.exp(jax.random.uniform(key_diag, (NSEP, B), minval=-0.7, maxval=0.7))
    off_part = jax.random.normal(key_off, (NSEP, B, B))
    return assemble(diagonal, off_part).astype(jnp.bfloat16)


def draw_leaf_links(key, part):
    key = jax.random.fold_in(key, 37)
    device_count = NLEAF // LEAF_DEV
    window = LEAF_DEV * K
    column_count = device_count // NSEP
    scores = jax.random.randint(key, (device_count, window), 0, 1 << 20) * window
    scores = scores + lax.broadcasted_iota(jnp.int32, (device_count, window), 1)
    ordering = jnp.argsort(scores, axis=1).astype(jnp.int32)
    near = ordering - window // 2
    offsets = jnp.where(ordering == window - 1, NSEP // 2, near).astype(jnp.int32)
    block_row = lax.broadcasted_iota(jnp.int32, (device_count, window), 0) // column_count
    chosen = (block_row + offsets + NSEP) % NSEP
    return chosen.reshape(NLEAF, K).astype(jnp.int32)


def level_of(rng, dims, cuts, low, high):
    def one(position, blocks):
        steps = jax.random.uniform(jax.random.fold_in(jax.random.fold_in(rng, 6), position), (blocks,), jnp.float32, low / len(cuts), high / len(cuts))
        return jnp.repeat(jnp.exp(steps), dims[position] // blocks).reshape((-1,) + (1,) * (len(dims) - position - 1))

    level = one(*cuts[0])
    for cut in cuts[1:]:
        level = level * one(*cut)
    return level


def centred(stream_key, dims, spread, bound, pieces=(), held_as=jnp.bfloat16):
    values = spread * jax.random.normal(stream_key, dims, jnp.float32)
    if pieces:
        values = values * level_of(stream_key, dims, pieces, -0.22, 0.18)
    return jnp.clip(values, -bound, bound).astype(held_as)


def setup_inputs(seed: int = 0) -> dict:
    arg_keys = jax.random.split(jax.random.key(seed), 7)
    return {
        "leaf_rhs": centred(arg_keys[0], (NLEAF, R, B), 1.0, 6.0, ((0, 512),)),
        "leaf_inverse": draw_leaf_inverse(jax.random.fold_in(arg_keys[6], 71), 0),
        "leaf_lower": centred(arg_keys[2], (NLEAF, K, B, B), (B * LEAF_DEV * N_PCOL * K) ** -0.5, 0.02734375, ((0, 512),)),
        "leaf_links": draw_leaf_links(jax.random.fold_in(arg_keys[6], 71), 0),
        "sep_rhs": centred(arg_keys[4], (NSEP, R, B), 1.0, 6.0, ((0, 64),)),
        "sep_inverse": draw_sep_inverse(jax.random.fold_in(arg_keys[6], 71), 0),
    }


def reference(leaf_rhs, leaf_inverse, leaf_lower, leaf_links, sep_rhs, sep_inverse):
    forward = jnp.einsum("lrb,lab->lra", leaf_rhs.astype(jnp.float32), leaf_inverse.astype(jnp.float32)).astype(jnp.bfloat16)

    def add_leaf(running, leaf_item):
        lower_blocks, forward_part, link_ids = leaf_item
        link_terms = jnp.einsum("kab,rb->kra", lower_blocks.astype(jnp.float32), forward_part.astype(jnp.float32))
        return running.at[link_ids].add(link_terms), None

    zero_sums = jnp.zeros((NSEP, R, B), jnp.float32)
    sep_sums, _ = lax.scan(add_leaf, zero_sums, (leaf_lower, forward, leaf_links))
    right_side = (sep_rhs.astype(jnp.float32) - sep_sums).astype(jnp.bfloat16)
    middle = jnp.einsum("srb,sab->sra", right_side.astype(jnp.float32), sep_inverse.astype(jnp.float32)).astype(jnp.bfloat16)
    sep_solution = jnp.einsum("sra,sac->src", middle.astype(jnp.float32), sep_inverse.astype(jnp.float32)).astype(jnp.bfloat16)

    def back_leaf(leaf_item):
        lower_blocks, forward_part, link_ids, inverse = leaf_item
        picked = sep_solution[link_ids].astype(jnp.float32)
        back_terms = jnp.einsum("kab,kra->rb", lower_blocks.astype(jnp.float32), picked)
        remainder = (forward_part.astype(jnp.float32) - back_terms).astype(jnp.bfloat16)
        return jnp.dot(remainder, inverse, preferred_element_type=jnp.float32).astype(jnp.bfloat16)

    leaf_solution = lax.map(back_leaf, (leaf_lower, forward, leaf_links, leaf_inverse))
    return leaf_solution, sep_solution
```

```python
import jax
import jax.numpy as jnp
from jax import lax
from jax.experimental import pallas as pl
from jax.experimental.pallas import tpu as pltpu
from jax.sharding import Mesh
from jax.sharding import PartitionSpec as P

NZ, NY, NX, NC = 16, 4, 4, 2
FACE = ("y", "x")
NFACE = NY * NX
REACH = 3
NSLOT = 8
R, B = 64, 256
RP = R // (NX * NC)
LANES = 128
CHUNKS = 8

F32, BF16 = jnp.float32, jnp.bfloat16
SMEM = pl.BlockSpec(memory_space=pltpu.SMEM)
VMEM = pl.BlockSpec(memory_space=pltpu.VMEM)
HBM = pl.BlockSpec(memory_space=pltpu.HBM)
PARAMS = pltpu.CompilerParams(vmem_limit_bytes=32 * 1024 * 1024)


def dot_nt(a, b):
    return lax.dot_general(a, b, (((1,), (1,)), ((), ())), preferred_element_type=F32)


def dot_nn(a, b):
    return lax.dot_general(a, b, (((1,), (0,)), ((), ())), preferred_element_type=F32)


def slot_of(link, z):
    plane_slot = jnp.minimum((link // NY - z + REACH + NZ) % NZ, NSLOT - 1)
    return (link % NY) * NSLOT + plane_slot


def plane_of(slot, z):
    return (z + (NZ // 2 if slot == NSLOT - 1 else slot - REACH) + NZ) % NZ


def rows_of(x, c):
    return pl.ds(pl.multiple_of((x * NC + c) * RP, RP), RP)


def fold(rows):
    return jnp.concatenate([rows[:, :LANES], rows[:, LANES:]], axis=0).astype(BF16)


def unfold(tile):
    tile = tile.astype(F32)
    return jnp.concatenate([tile[:RP], tile[RP:]], axis=1)


def link_kernel(at_ref, links_ref, rhs_ref, inverse_ref, lower_hbm, forward_ref, keep_ref, send_ref, lower_ref, terms_ref, sems):
    leaves, links = links_ref.shape
    per = leaves * links // CHUNKS
    copies = [
        pltpu.make_async_copy(lower_hbm.at[pl.ds(n * per, per)], lower_ref.at[pl.ds(n * per, per)], sems.at[n])
        for n in range(CHUNKS)
    ]
    for copy in copies:
        copy.start()
    z, c = at_ref[0], at_ref[3]
    terms_ref[...] = jnp.zeros_like(terms_ref)
    for i in range(leaves):
        forward = dot_nt(rhs_ref[i], inverse_ref[i]).astype(BF16)
        forward_ref[i] = forward
        for k in range(links):
            n = i * links + k
            if n % per == 0:
                copies[n // per].wait()
            terms_ref[slot_of(links_ref[i, k], z)] = dot_nt(forward, lower_ref[n])
    for y in range(NY):
        for x in range(NX):
            mine = terms_ref[y * NSLOT:(y + 1) * NSLOT, rows_of(x, c), :]
            keep_ref[y * NX + x] = mine.reshape(NSLOT * RP, B)
            other = terms_ref[y * NSLOT:(y + 1) * NSLOT, rows_of(x, 1 - c), :]
            send_ref[y * NX + x] = other.reshape(NSLOT * RP, B).astype(BF16)


def pair_kernel(keep_ref, part_ref, out_ref):
    out_ref[...] = (keep_ref[...] + part_ref[...].astype(F32)).astype(BF16)


def face_kernel(at_ref, parts_ref, out_ref):
    z = at_ref[0]
    total = parts_ref[0].astype(F32)
    for n in range(1, NFACE):
        total = total + parts_ref[n].astype(F32)
    out_ref[...] = jnp.zeros_like(out_ref)
    for slot in range(NSLOT):
        out_ref[plane_of(slot, z)] = fold(total[slot * RP:(slot + 1) * RP])


def solve_kernel(at_ref, parts_ref, rhs_ref, inverse_ref, out_ref, rhs32_ref):
    rhs32_ref[...] = rhs_ref[0].astype(F32)
    sums = parts_ref[0].astype(F32)
    for n in range(1, NZ):
        sums = sums + parts_ref[n].astype(F32)
    sums = jnp.concatenate([sums[:RP], sums[RP:]], axis=1)
    right_side = (rhs32_ref[rows_of(at_ref[2], at_ref[3]), :] - sums).astype(BF16)
    middle = dot_nt(right_side, inverse_ref[0]).astype(BF16)
    solved = dot_nn(middle, inverse_ref[0])
    out_ref[...] = jnp.broadcast_to(fold(solved)[None], out_ref.shape)


def pick_kernel(at_ref, planes_ref, out_ref):
    z = at_ref[0]
    picked = jnp.concatenate([unfold(planes_ref[plane_of(slot, z)]) for slot in range(NSLOT)], axis=0)
    out_ref[...] = jnp.broadcast_to(picked.astype(BF16)[None], out_ref.shape)


def back_kernel(at_ref, links_ref, mine_ref, other_ref, lower_ref, forward_ref, inverse_ref, leaf_ref, sep_ref, seps_ref, rows_ref):
    z, row, c = at_ref[0], at_ref[1], at_ref[3]
    leaves, links = links_ref.shape
    for y in range(NY):
        for x in range(NX):
            mine = mine_ref[y * NX + x].astype(F32).reshape(NSLOT, RP, B)
            seps_ref[y * NSLOT:(y + 1) * NSLOT, rows_of(x, c), :] = mine
            other = other_ref[y * NX + x].astype(F32).reshape(NSLOT, RP, B)
            seps_ref[y * NSLOT:(y + 1) * NSLOT, rows_of(x, 1 - c), :] = other
    sep_ref[0] = seps_ref[row * NSLOT + REACH].astype(BF16)
    for i in range(leaves):
        for k in range(links):
            rows_ref[:, k * B:(k + 1) * B] = seps_ref[slot_of(links_ref[i, k], z)].astype(BF16)
        back_terms = dot_nn(rows_ref[...], lower_ref[i])
        remainder = (forward_ref[i].astype(F32) - back_terms).astype(BF16)
        leaf_ref[i] = dot_nn(remainder, inverse_ref[i]).astype(BF16)


def call(kernel, outs, in_specs, scratch=()):
    many = isinstance(outs, tuple)
    return pl.pallas_call(
        kernel,
        out_shape=outs,
        in_specs=in_specs,
        out_specs=tuple(VMEM for _ in outs) if many else VMEM,
        scratch_shapes=scratch,
        compiler_params=PARAMS,
    )


def shards(leaf_rhs, leaf_inverse, leaf_lower, leaf_links, sep_rhs, sep_inverse):
    leaves, links = leaf_links.shape
    at = jnp.stack([lax.axis_index(a) for a in ("z", "y", "x", "c")]).astype(jnp.int32)
    shape = jax.ShapeDtypeStruct
    swap = [(0, 1), (1, 0)]
    face = (NFACE, NSLOT * RP, B)
    column = (NZ, 2 * RP, LANES)
    forward, keep, send = call(
        link_kernel,
        (shape((leaves, R, B), BF16), shape(face, F32), shape(face, BF16)),
        [SMEM, SMEM, VMEM, VMEM, HBM],
        (
            pltpu.VMEM((leaves * links, B, B), BF16),
            pltpu.VMEM((NY * NSLOT, R, B), F32),
            pltpu.SemaphoreType.DMA((CHUNKS,)),
        ),
    )(at, leaf_links, leaf_rhs, leaf_inverse, leaf_lower.reshape(leaves * links, B, B))
    part = lax.ppermute(send, "c", swap)
    pairs = call(pair_kernel, shape(face, BF16), [VMEM, VMEM])(keep, part)
    parts = lax.all_to_all(pairs, FACE, 0, 0, tiled=True)
    sums = call(face_kernel, shape(column, BF16), [SMEM, VMEM])(at, parts)
    parts = lax.all_to_all(sums, "z", 0, 0, tiled=True)
    solved = call(
        solve_kernel, shape(column, BF16), [SMEM, VMEM, VMEM, VMEM], (pltpu.VMEM((R, B), F32),)
    )(at, parts, sep_rhs, sep_inverse)
    planes = lax.all_to_all(solved, "z", 0, 0, tiled=True)
    picked = call(pick_kernel, shape(face, BF16), [SMEM, VMEM])(at, planes)
    mine = lax.all_to_all(picked, FACE, 0, 0, tiled=True)
    other = lax.ppermute(mine, "c", swap)
    return call(
        back_kernel,
        (shape((leaves, R, B), BF16), shape((1, R, B), BF16)),
        [SMEM, SMEM] + [VMEM] * 5,
        (pltpu.VMEM((NY * NSLOT, R, B), F32), pltpu.VMEM((R, links * B), BF16)),
    )(at, leaf_links, mine, other, leaf_lower.reshape(leaves, links * B, B), forward, leaf_inverse)


def solution(mesh):
    grid = Mesh(mesh.devices.reshape(NZ, NY, NX, NC), ("z", "y", "x", "c"))
    every, row = ("z", "y", "x", "c"), ("z", "y")
    return jax.shard_map(
        shards,
        mesh=grid,
        in_specs=(P(every), P(every), P(every), P(every), P(row), P(row)),
        out_specs=(P(every), P(row)),
        check_vma=False,
    )
```

```python
import jax
import jax.numpy as jnp
from jax import lax
from jax.experimental import pallas as pl
from jax.experimental.pallas import tpu as pltpu
from jax.sharding import Mesh
from jax.sharding import PartitionSpec as P

NZ, NY, NX, NC = 16, 4, 4, 2
FACE = ("y", "x")
NFACE = NY * NX
REACH = 3
NSLOT = 8
R, B = 64, 256
RP = R // (NX * NC)
RH = R // NC
LANES = 128
CHUNKS = 8

F32, BF16 = jnp.float32, jnp.bfloat16
SMEM = pl.BlockSpec(memory_space=pltpu.SMEM)
VMEM = pl.BlockSpec(memory_space=pltpu.VMEM)
HBM = pl.BlockSpec(memory_space=pltpu.HBM)
PARAMS = pltpu.CompilerParams(vmem_limit_bytes=32 * 1024 * 1024)


def dot_nt(a, b):
    return lax.dot_general(a, b, (((1,), (1,)), ((), ())), preferred_element_type=F32)


def dot_nn(a, b):
    return lax.dot_general(a, b, (((1,), (0,)), ((), ())), preferred_element_type=F32)


def slot_of(link, z):
    plane_slot = jnp.minimum((link // NY - z + REACH + NZ) % NZ, NSLOT - 1)
    return (link % NY) * NSLOT + plane_slot


def plane_of(slot, z):
    return (z + (NZ // 2 if slot == NSLOT - 1 else slot - REACH) + NZ) % NZ


def rows_of(x, c):
    return pl.ds(pl.multiple_of((c * NX + x) * RP, RP), RP)


def fold(rows):
    return jnp.concatenate([rows[:, :LANES], rows[:, LANES:]], axis=0).astype(BF16)


def unfold(tile):
    tile = tile.astype(F32)
    return jnp.concatenate([tile[:RP], tile[RP:]], axis=1)


def link_kernel(at_ref, links_hbm, rhs_hbm, inverse_hbm, lower_hbm, forward_ref, keep_ref, send_ref,
                links_ref, rhs_ref, inverse_ref, lower_ref, terms_ref, sems):
    leaves, links = links_ref.shape
    per = leaves * links // CHUNKS
    copies = [
        pltpu.make_async_copy(links_hbm, links_ref, sems.at[CHUNKS]),
        pltpu.make_async_copy(rhs_hbm, rhs_ref, sems.at[CHUNKS + 1]),
        pltpu.make_async_copy(inverse_hbm, inverse_ref, sems.at[CHUNKS + 2]),
    ] + [
        pltpu.make_async_copy(lower_hbm.at[pl.ds(n * per, per)], lower_ref.at[pl.ds(n * per, per)], sems.at[n])
        for n in range(CHUNKS)
    ]
    for copy in copies:
        copy.start()
    small, blocks = copies[:3], copies[3:]
    z, c = at_ref[0], at_ref[3]
    terms_ref[...] = jnp.zeros_like(terms_ref)
    for copy in small:
        copy.wait()
    for i in range(leaves):
        forward_ref[i] = dot_nt(rhs_ref[i], inverse_ref[i]).astype(BF16).reshape(NC, RH, B)
    for i in range(leaves):
        forward = forward_ref[i].reshape(R, B)
        for k in range(links):
            n = i * links + k
            if n % per == 0:
                blocks[n // per].wait()
            terms_ref[slot_of(links_ref[i, k], z)] = dot_nt(forward, lower_ref[n])
    for y in range(NY):
        for x in range(NX):
            mine = terms_ref[y * NSLOT:(y + 1) * NSLOT, rows_of(x, c), :]
            keep_ref[y * NX + x] = mine.reshape(NSLOT * RP, B)
            other = terms_ref[y * NSLOT:(y + 1) * NSLOT, rows_of(x, 1 - c), :]
            send_ref[y * NX + x] = other.reshape(NSLOT * RP, B).astype(BF16)


def pair_kernel(keep_ref, part_ref, out_ref):
    out_ref[...] = (keep_ref[...] + part_ref[...].astype(F32)).astype(BF16)


def face_kernel(at_ref, parts_ref, out_ref):
    z = at_ref[0]
    total = parts_ref[0].astype(F32)
    for n in range(1, NFACE):
        total = total + parts_ref[n].astype(F32)
    out_ref[...] = jnp.zeros_like(out_ref)
    for slot in range(NSLOT):
        out_ref[plane_of(slot, z)] = fold(total[slot * RP:(slot + 1) * RP])


def solve_kernel(at_ref, parts_ref, rhs_ref, inverse_ref, out_ref, rhs32_ref):
    rhs32_ref[...] = rhs_ref[0].astype(F32)
    sums = parts_ref[0].astype(F32)
    for n in range(1, NZ):
        sums = sums + parts_ref[n].astype(F32)
    sums = jnp.concatenate([sums[:RP], sums[RP:]], axis=1)
    right_side = (rhs32_ref[rows_of(at_ref[2], at_ref[3]), :] - sums).astype(BF16)
    middle = dot_nt(right_side, inverse_ref[0]).astype(BF16)
    solved = dot_nn(middle, inverse_ref[0])
    out_ref[...] = jnp.broadcast_to(fold(solved)[None], out_ref.shape)


def pick_kernel(at_ref, planes_ref, out_ref):
    z = at_ref[0]
    picked = jnp.concatenate([unfold(planes_ref[plane_of(slot, z)]) for slot in range(NSLOT)], axis=0)
    out_ref[...] = jnp.broadcast_to(picked.astype(BF16)[None], out_ref.shape)


def back_half(z, row, links_ref, parts_ref, lower_ref, forward_ref, inverse_ref, seps_ref, rows_ref, half):
    leaves, links = links_ref.shape
    for y in range(NY):
        for x in range(NX):
            part = parts_ref[y * NX + x].astype(F32).reshape(NSLOT, RP, B)
            seps_ref[y * NSLOT:(y + 1) * NSLOT, x * RP:(x + 1) * RP, :] = part
    solved = []
    for i in range(leaves):
        for k in range(links):
            rows_ref[:, k * B:(k + 1) * B] = seps_ref[slot_of(links_ref[i, k], z)].astype(BF16)
        back_terms = dot_nn(rows_ref[...], lower_ref[i])
        remainder = (forward_ref[i, half].astype(F32) - back_terms).astype(BF16)
        solved.append(dot_nn(remainder, inverse_ref[i]).astype(BF16))
    return solved, seps_ref[row * NSLOT + REACH].astype(BF16)


def mine_kernel(at_ref, links_ref, parts_ref, lower_ref, forward_ref, inverse_ref, leaf_ref, sep_ref, seps_ref, rows_ref):
    solved, sep = back_half(at_ref[0], at_ref[1], links_ref, parts_ref, lower_ref, forward_ref, inverse_ref,
                            seps_ref, rows_ref, at_ref[3])
    for i, rows in enumerate(solved):
        leaf_ref[i] = rows
    sep_ref[...] = sep


def other_kernel(at_ref, links_ref, parts_ref, lower_ref, forward_ref, inverse_ref, leaf_half_ref, sep_half_ref,
                 leaf_ref, sep_ref, seps_ref, rows_ref):
    c = at_ref[3]
    solved, sep = back_half(at_ref[0], at_ref[1], links_ref, parts_ref, lower_ref, forward_ref, inverse_ref,
                            seps_ref, rows_ref, 1 - c)
    for i, rows in enumerate(solved):
        leaf_ref[i, c] = leaf_half_ref[i]
        leaf_ref[i, 1 - c] = rows
    sep_ref[0, c] = sep_half_ref[...]
    sep_ref[0, 1 - c] = sep


def stay(array):
    return pltpu.with_memory_space_constraint(array, pltpu.HBM)


def call(kernel, outs, in_specs, scratch=()):
    many = isinstance(outs, tuple)
    return pl.pallas_call(
        kernel,
        out_shape=outs,
        in_specs=in_specs,
        out_specs=tuple(VMEM for _ in outs) if many else VMEM,
        scratch_shapes=scratch,
        compiler_params=PARAMS,
    )


def shards(leaf_rhs, leaf_inverse, leaf_lower, leaf_links, sep_rhs, sep_inverse):
    leaves, links = leaf_links.shape
    at = jnp.stack([lax.axis_index(a) for a in ("z", "y", "x", "c")]).astype(jnp.int32)
    shape = jax.ShapeDtypeStruct
    swap = [(0, 1), (1, 0)]
    face = (NFACE, NSLOT * RP, B)
    column = (NZ, 2 * RP, LANES)
    forward, keep, send = call(
        link_kernel,
        (shape((leaves, NC, RH, B), BF16), shape(face, F32), shape(face, BF16)),
        [SMEM, HBM, HBM, HBM, HBM],
        (
            pltpu.SMEM((leaves, links), jnp.int32),
            pltpu.VMEM((leaves, R, B), BF16),
            pltpu.VMEM((leaves, B, B), BF16),
            pltpu.VMEM((leaves * links, B, B), BF16),
            pltpu.VMEM((NY * NSLOT, R, B), F32),
            pltpu.SemaphoreType.DMA((CHUNKS + 3,)),
        ),
    )(at, *map(stay, (leaf_links, leaf_rhs, leaf_inverse, leaf_lower.reshape(leaves * links, B, B))))
    part = lax.ppermute(send, "c", swap)
    pairs = call(pair_kernel, shape(face, BF16), [VMEM, VMEM])(keep, part)
    parts = lax.all_to_all(pairs, FACE, 0, 0, tiled=True)
    sums = call(face_kernel, shape(column, BF16), [SMEM, VMEM])(at, parts)
    parts = lax.all_to_all(sums, "z", 0, 0, tiled=True)
    solved = call(
        solve_kernel, shape(column, BF16), [SMEM, VMEM, VMEM, VMEM], (pltpu.VMEM((R, B), F32),)
    )(at, parts, sep_rhs, sep_inverse)
    planes = lax.all_to_all(solved, "z", 0, 0, tiled=True)
    picked = call(pick_kernel, shape(face, BF16), [SMEM, VMEM])(at, planes)
    mine = lax.all_to_all(picked, FACE, 0, 0, tiled=True)
    other = lax.ppermute(mine, "c", swap)
    lower = leaf_lower.reshape(leaves, links * B, B)
    scratch = (pltpu.VMEM((NY * NSLOT, RH, B), F32), pltpu.VMEM((RH, links * B), BF16))
    halves = call(
        mine_kernel, (shape((leaves, RH, B), BF16), shape((RH, B), BF16)), [SMEM, SMEM] + [VMEM] * 4, scratch
    )(at, leaf_links, mine, lower, forward, leaf_inverse)
    leaf_solution, sep_solution = call(
        other_kernel,
        (shape((leaves, NC, RH, B), BF16), shape((1, NC, RH, B), BF16)),
        [SMEM, SMEM] + [VMEM] * 6,
        scratch,
    )(at, leaf_links, other, lower, forward, leaf_inverse, *halves)
    return leaf_solution.reshape(leaves, R, B), sep_solution.reshape(1, R, B)


def solution(mesh):
    grid = Mesh(mesh.devices.reshape(NZ, NY, NX, NC), ("z", "y", "x", "c"))
    every, row = ("z", "y", "x", "c"), ("z", "y")
    return jax.shard_map(
        shards,
        mesh=grid,
        in_specs=(P(every), P(every), P(every), P(every), P(row), P(row)),
        out_specs=(P(every), P(row)),
        check_vma=False,
    )
```

```python
import jax
import jax.numpy as jnp
from jax import lax
from jax.experimental import pallas as pl
from jax.experimental.pallas import tpu as pltpu
from jax.sharding import Mesh
from jax.sharding import PartitionSpec as P

NZ, NY, NX, NC = 16, 4, 4, 2
FACE = ("y", "x")
NFACE = NY * NX
NEAR = (-2, -1, 0, 1, 2)
OWN, EDGE, FAR = 2, 5, 6
NSLOT = 7
R, B = 64, 256
RP = R // (NX * NC)
RH = R // NC
LANES = 128
CHUNKS = 3

F32, BF16 = jnp.float32, jnp.bfloat16
VMEM = pl.BlockSpec(memory_space=pltpu.VMEM)
HBM = pl.BlockSpec(memory_space=pltpu.HBM)
PARAMS = pltpu.CompilerParams(vmem_limit_bytes=32 * 1024 * 1024)


def dot_nt(a, b):
    return lax.dot_general(a, b, (((1,), (1,)), ((), ())), preferred_element_type=F32)


def dot_nn(a, b):
    return lax.dot_general(a, b, (((1,), (0,)), ((), ())), preferred_element_type=F32)


def slot_of(link, z):
    step = (link // NY - z - NEAR[0] + NZ) % NZ
    plane_slot = jnp.where(step <= EDGE, step, jnp.where(step == NZ - 1, EDGE, FAR))
    return (link % NY) * NSLOT + plane_slot


def plane_of(step, z):
    return (z + step + NZ) % NZ


def rows_of(x, c):
    return pl.ds(pl.multiple_of((c * NX + x) * RP, RP), RP)


def fold(rows):
    return jnp.concatenate([rows[..., :LANES], rows[..., LANES:]], axis=-2)


def unfold(tile):
    return jnp.concatenate([tile[..., :RP, :], tile[..., RP:, :]], axis=-1)


def link_kernel(links_hbm, rhs_hbm, inverse_hbm, lower_hbm, forward_ref, keep_ref, send_ref,
                links_ref, rhs_ref, inverse_ref, lower_ref, terms_ref, sems):
    leaves, links = links_ref.shape
    per = leaves * links // CHUNKS
    copies = [
        pltpu.make_async_copy(links_hbm, links_ref, sems.at[CHUNKS]),
        pltpu.make_async_copy(rhs_hbm, rhs_ref, sems.at[CHUNKS + 1]),
        pltpu.make_async_copy(inverse_hbm, inverse_ref, sems.at[CHUNKS + 2]),
    ] + [
        pltpu.make_async_copy(lower_hbm.at[pl.ds(n * per, per)], lower_ref.at[pl.ds(n * per, per)], sems.at[n])
        for n in range(CHUNKS)
    ]
    for copy in copies:
        copy.start()
    small, blocks = copies[1:3], copies[3:]
    z, c = lax.axis_index("z"), lax.axis_index("c")
    terms_ref[...] = jnp.zeros_like(terms_ref)
    for copy in small:
        copy.wait()
    for i in range(leaves):
        forward_ref[i] = dot_nt(rhs_ref[i], inverse_ref[i]).astype(BF16).reshape(NC, RH, B)
    copies[0].wait()
    for i in range(leaves):
        forward = forward_ref[i].reshape(R, B)
        for k in range(links):
            n = i * links + k
            if n % per == 0:
                blocks[n // per].wait()
            terms_ref[slot_of(links_ref[i, k], z)] = dot_nt(forward, lower_ref[n])
    for y in range(NY):
        for x in range(NX):
            slots = slice(y * NSLOT, (y + 1) * NSLOT)
            mine = fold(terms_ref[slots, rows_of(x, c), :])
            keep_ref[y * NX + x] = mine.reshape(NSLOT * 2 * RP, LANES)
            other = fold(terms_ref[slots, rows_of(x, 1 - c), :])
            send_ref[y * NX + x] = other.reshape(NSLOT * 2 * RP, LANES).astype(BF16)


def pair_kernel(keep_ref, part_ref, out_ref):
    out_ref[...] = (keep_ref[...] + part_ref[...].astype(F32)).astype(BF16)


def face_kernel(parts_ref, out_ref):
    z, y = lax.axis_index("z"), lax.axis_index("y")
    rows = []
    for w in range(NY):
        total = parts_ref[w * NX].astype(F32)
        for x in range(1, NX):
            total = total + parts_ref[w * NX + x].astype(F32)
        rows.append(total.reshape(NSLOT, 2 * RP, LANES))
    total = rows[0] + rows[1] + rows[2] + rows[3]
    below = rows[0][EDGE]
    for w in range(1, NY):
        below = below + jnp.where(w <= y, rows[w][EDGE], 0.0)
    above = jnp.zeros_like(below)
    for w in range(1, NY):
        above = above + jnp.where(w > y, rows[w][EDGE], 0.0)
    out_ref[...] = jnp.zeros_like(out_ref)
    for slot, step in enumerate(NEAR):
        out_ref[plane_of(step, z)] = total[slot].astype(BF16)
    out_ref[plane_of(-3, z)] = below.astype(BF16)
    out_ref[plane_of(3, z)] = above.astype(BF16)
    out_ref[plane_of(NZ // 2, z)] = total[FAR].astype(BF16)


def solve_kernel(parts_ref, rhs_ref, inverse_ref, out_ref, rhs32_ref):
    rhs32_ref[...] = rhs_ref[0].astype(F32)
    sums = parts_ref[0].astype(F32)
    for n in range(1, NZ):
        sums = sums + parts_ref[n].astype(F32)
    right_side = (rhs32_ref[rows_of(lax.axis_index("x"), lax.axis_index("c")), :] - unfold(sums)).astype(BF16)
    middle = dot_nt(right_side, inverse_ref[0]).astype(BF16)
    solved = dot_nn(middle, inverse_ref[0])
    out_ref[...] = jnp.broadcast_to(fold(solved).astype(BF16)[None], out_ref.shape)


def pick_kernel(planes_ref, out_ref):
    z, y = lax.axis_index("z"), lax.axis_index("y")
    near = [planes_ref[plane_of(step, z)] for step in NEAR]
    below, above, far = (planes_ref[plane_of(step, z)] for step in (-3, 3, NZ // 2))
    for w in range(NY):
        edge = jnp.where(w <= y, below.astype(F32), above.astype(F32)).astype(BF16)
        picked = jnp.concatenate(near + [edge, far], axis=0)
        for x in range(NX):
            out_ref[w * NX + x] = picked


def back_half(links_hbm, parts_ref, lower_ref, forward_ref, inverse_ref, links_ref, seps_ref, rows_ref, sem, half):
    leaves, links = links_ref.shape
    z, y = lax.axis_index("z"), lax.axis_index("y")
    copy = pltpu.make_async_copy(links_hbm, links_ref, sem)
    copy.start()
    for w in range(NY):
        for x in range(NX):
            part = parts_ref[w * NX + x].astype(F32).reshape(NSLOT, 2 * RP, LANES)
            seps_ref[w * NSLOT:(w + 1) * NSLOT, x * RP:(x + 1) * RP, :] = unfold(part)
    copy.wait()
    solved = []
    for i in range(leaves):
        for k in range(links):
            rows_ref[:, k * B:(k + 1) * B] = seps_ref[slot_of(links_ref[i, k], z)].astype(BF16)
        back_terms = dot_nn(rows_ref[...], lower_ref[i])
        remainder = (forward_ref[i, half].astype(F32) - back_terms).astype(BF16)
        solved.append(dot_nn(remainder, inverse_ref[i]).astype(BF16))
    return solved, seps_ref[y * NSLOT + OWN].astype(BF16)


def mine_kernel(links_hbm, parts_ref, lower_ref, forward_ref, inverse_ref, leaf_ref, sep_ref, *scratch):
    c = lax.axis_index("c")
    solved, sep = back_half(links_hbm, parts_ref, lower_ref, forward_ref, inverse_ref, *scratch, c)
    for i, rows in enumerate(solved):
        leaf_ref[i] = rows
    sep_ref[...] = sep


def other_kernel(links_hbm, parts_ref, lower_ref, forward_ref, inverse_ref, leaf_half_ref, sep_half_ref,
                 leaf_ref, sep_ref, *scratch):
    c = lax.axis_index("c")
    solved, sep = back_half(links_hbm, parts_ref, lower_ref, forward_ref, inverse_ref, *scratch, 1 - c)
    for i, rows in enumerate(solved):
        leaf_ref[i, c] = leaf_half_ref[i]
        leaf_ref[i, 1 - c] = rows
    sep_ref[0, c] = sep_half_ref[...]
    sep_ref[0, 1 - c] = sep


def stay(array):
    return pltpu.with_memory_space_constraint(array, pltpu.HBM)


def call(kernel, outs, in_specs, scratch=()):
    many = isinstance(outs, tuple)
    return pl.pallas_call(
        kernel,
        out_shape=outs,
        in_specs=in_specs,
        out_specs=tuple(VMEM for _ in outs) if many else VMEM,
        scratch_shapes=scratch,
        compiler_params=PARAMS,
    )


def shards(leaf_rhs, leaf_inverse, leaf_lower, leaf_links, sep_rhs, sep_inverse):
    leaves, links = leaf_links.shape
    shape = jax.ShapeDtypeStruct
    swap = [(0, 1), (1, 0)]
    face = (NFACE, NSLOT * 2 * RP, LANES)
    column = (NZ, 2 * RP, LANES)
    forward, keep, send = call(
        link_kernel,
        (shape((leaves, NC, RH, B), BF16), shape(face, F32), shape(face, BF16)),
        [HBM, HBM, HBM, HBM],
        (
            pltpu.SMEM((leaves, links), jnp.int32),
            pltpu.VMEM((leaves, R, B), BF16),
            pltpu.VMEM((leaves, B, B), BF16),
            pltpu.VMEM((leaves * links, B, B), BF16),
            pltpu.VMEM((NY * NSLOT, R, B), F32),
            pltpu.SemaphoreType.DMA((CHUNKS + 3,)),
        ),
    )(*map(stay, (leaf_links, leaf_rhs, leaf_inverse, leaf_lower.reshape(leaves * links, B, B))))
    part = lax.ppermute(send, "c", swap)
    pairs = call(pair_kernel, shape(face, BF16), [VMEM, VMEM])(keep, part)
    parts = lax.all_to_all(pairs, FACE, 0, 0, tiled=True)
    sums = call(face_kernel, shape(column, BF16), [VMEM])(parts)
    parts = lax.all_to_all(sums, "z", 0, 0, tiled=True)
    solved = call(
        solve_kernel, shape(column, BF16), [VMEM, VMEM, VMEM], (pltpu.VMEM((R, B), F32),)
    )(parts, sep_rhs, sep_inverse)
    planes = lax.all_to_all(solved, "z", 0, 0, tiled=True)
    picked = call(pick_kernel, shape(face, BF16), [VMEM])(planes)
    mine = lax.all_to_all(picked, FACE, 0, 0, tiled=True)
    other = lax.ppermute(mine, "c", swap)
    lower = leaf_lower.reshape(leaves, links * B, B)
    scratch = (
        pltpu.SMEM((leaves, links), jnp.int32),
        pltpu.VMEM((NY * NSLOT, RH, B), F32),
        pltpu.VMEM((RH, links * B), BF16),
        pltpu.SemaphoreType.DMA(()),
    )
    halves = call(
        mine_kernel, (shape((leaves, RH, B), BF16), shape((RH, B), BF16)), [HBM] + [VMEM] * 4, scratch
    )(stay(leaf_links), mine, lower, forward, leaf_inverse)
    leaf_solution, sep_solution = call(
        other_kernel,
        (shape((leaves, NC, RH, B), BF16), shape((1, NC, RH, B), BF16)),
        [HBM] + [VMEM] * 6,
        scratch,
    )(stay(leaf_links), other, lower, forward, leaf_inverse, *halves)
    return leaf_solution.reshape(leaves, R, B), sep_solution.reshape(1, R, B)


def solution(mesh):
    grid = Mesh(mesh.devices.reshape(NZ, NY, NX, NC), ("z", "y", "x", "c"))
    every, row = ("z", "y", "x", "c"), ("z", "y")
    return jax.shard_map(
        shards,
        mesh=grid,
        in_specs=(P(every), P(every), P(every), P(every), P(row), P(row)),
        out_specs=(P(every), P(row)),
        check_vma=False,
    )
```

```python
import jax
import jax.numpy as jnp
from jax import lax
from jax.experimental import pallas as pl
from jax.experimental.pallas import tpu as pltpu
from jax.sharding import Mesh
from jax.sharding import PartitionSpec as P

NZ, NY, NX, NC = 16, 4, 4, 2
FACE = ("y", "x")
NFACE = NY * NX
NEAR = (-2, -1, 0, 1, 2)
OWN, EDGE, FAR = 2, 5, 6
NSLOT = 7
R, B = 64, 256
RP = R // (NX * NC)
LANES = 128
CHUNKS = 3

F32, BF16 = jnp.float32, jnp.bfloat16
VMEM = pl.BlockSpec(memory_space=pltpu.VMEM)
HBM = pl.BlockSpec(memory_space=pltpu.HBM)
PARAMS = pltpu.CompilerParams(vmem_limit_bytes=32 * 1024 * 1024)


def dot_nt(a, b):
    return lax.dot_general(a, b, (((1,), (1,)), ((), ())), preferred_element_type=F32)


def dot_nn(a, b):
    return lax.dot_general(a, b, (((1,), (0,)), ((), ())), preferred_element_type=F32)


def slot_of(link, z):
    step = (link // NY - z - NEAR[0] + NZ) % NZ
    plane_slot = jnp.where(step <= EDGE, step, jnp.where(step == NZ - 1, EDGE, FAR))
    return (link % NY) * NSLOT + plane_slot


def plane_of(step, z):
    return (z + step + NZ) % NZ


def rows_of(x, c):
    return pl.ds(pl.multiple_of((c * NX + x) * RP, RP), RP)


def fold(rows):
    return jnp.concatenate([rows[..., :LANES], rows[..., LANES:]], axis=-2)


def unfold(tile):
    return jnp.concatenate([tile[..., :RP, :], tile[..., RP:, :]], axis=-1)


def link_kernel(links_hbm, rhs_hbm, inverse_hbm, lower_hbm, forward_ref, keep_ref, send_ref,
                links_ref, rhs_ref, inverse_ref, lower_ref, terms_ref, sems):
    leaves, links = links_ref.shape
    per = leaves * links // CHUNKS
    copies = [
        pltpu.make_async_copy(links_hbm, links_ref, sems.at[CHUNKS]),
        pltpu.make_async_copy(rhs_hbm, rhs_ref, sems.at[CHUNKS + 1]),
        pltpu.make_async_copy(inverse_hbm, inverse_ref, sems.at[CHUNKS + 2]),
    ] + [
        pltpu.make_async_copy(lower_hbm.at[pl.ds(n * per, per)], lower_ref.at[pl.ds(n * per, per)], sems.at[n])
        for n in range(CHUNKS)
    ]
    for copy in copies:
        copy.start()
    small, blocks = copies[1:3], copies[3:]
    z, c = lax.axis_index("z"), lax.axis_index("c")
    terms_ref[...] = jnp.zeros_like(terms_ref)
    for copy in small:
        copy.wait()
    for i in range(leaves):
        forward_ref[i] = dot_nt(rhs_ref[i], inverse_ref[i]).astype(BF16)
    copies[0].wait()
    for i in range(leaves):
        forward = forward_ref[i]
        for k in range(links):
            n = i * links + k
            if n % per == 0:
                blocks[n // per].wait()
            terms_ref[slot_of(links_ref[i, k], z)] = dot_nt(forward, lower_ref[n])
    for y in range(NY):
        for x in range(NX):
            slots = slice(y * NSLOT, (y + 1) * NSLOT)
            mine = fold(terms_ref[slots, rows_of(x, c), :])
            keep_ref[y * NX + x] = mine.reshape(NSLOT * 2 * RP, LANES)
            other = fold(terms_ref[slots, rows_of(x, 1 - c), :])
            send_ref[y * NX + x] = other.reshape(NSLOT * 2 * RP, LANES).astype(BF16)


def pair_kernel(keep_ref, sent_ref, out_ref):
    out_ref[...] = (keep_ref[...] + sent_ref[1 - lax.axis_index("c")].astype(F32)).astype(BF16)


def face_kernel(parts_ref, out_ref):
    z, y = lax.axis_index("z"), lax.axis_index("y")
    rows = []
    for w in range(NY):
        total = parts_ref[w * NX].astype(F32)
        for x in range(1, NX):
            total = total + parts_ref[w * NX + x].astype(F32)
        rows.append(total.reshape(NSLOT, 2 * RP, LANES))
    total = rows[0] + rows[1] + rows[2] + rows[3]
    below = rows[0][EDGE]
    for w in range(1, NY):
        below = below + jnp.where(w <= y, rows[w][EDGE], 0.0)
    above = jnp.zeros_like(below)
    for w in range(1, NY):
        above = above + jnp.where(w > y, rows[w][EDGE], 0.0)
    out_ref[...] = jnp.zeros_like(out_ref)
    for slot, step in enumerate(NEAR):
        out_ref[plane_of(step, z)] = total[slot].astype(BF16)
    out_ref[plane_of(-3, z)] = below.astype(BF16)
    out_ref[plane_of(3, z)] = above.astype(BF16)
    out_ref[plane_of(NZ // 2, z)] = total[FAR].astype(BF16)


def solve_kernel(parts_ref, rhs_ref, inverse_ref, out_ref, rhs32_ref):
    rhs32_ref[...] = rhs_ref[0].astype(F32)
    sums = parts_ref[0].astype(F32)
    for n in range(1, NZ):
        sums = sums + parts_ref[n].astype(F32)
    right_side = (rhs32_ref[rows_of(lax.axis_index("x"), lax.axis_index("c")), :] - unfold(sums)).astype(BF16)
    middle = dot_nt(right_side, inverse_ref[0]).astype(BF16)
    solved = dot_nn(middle, inverse_ref[0])
    out_ref[...] = jnp.broadcast_to(fold(solved).astype(BF16)[None], out_ref.shape)


def pick_kernel(planes_ref, out_ref):
    z, y = lax.axis_index("z"), lax.axis_index("y")
    near = [planes_ref[plane_of(step, z)] for step in NEAR]
    below, above, far = (planes_ref[plane_of(step, z)] for step in (-3, 3, NZ // 2))
    for w in range(NY):
        edge = jnp.where(w <= y, below.astype(F32), above.astype(F32)).astype(BF16)
        picked = jnp.concatenate(near + [edge, far], axis=0)
        for x in range(NX):
            out_ref[w * NX + x] = picked


def back_kernel(links_vmem, parts_ref, lower_ref, forward_ref, inverse_ref, leaf_ref, sep_ref,
                links_ref, seps_ref, sem):
    leaves, links = links_ref.shape
    copy = pltpu.make_async_copy(links_vmem, links_ref, sem)
    copy.start()
    z, y = lax.axis_index("z"), lax.axis_index("y")
    for w in range(NY):
        for r in range(NC * NX):
            part = parts_ref[r // NX, w * NX + r % NX].astype(F32).reshape(NSLOT, 2 * RP, LANES)
            seps_ref[w * NSLOT:(w + 1) * NSLOT, r * RP:(r + 1) * RP, :] = unfold(part)
    sep_ref[0] = seps_ref[y * NSLOT + OWN].astype(BF16)
    copy.wait()
    for i in range(leaves):
        back_terms = jnp.zeros((R, B), F32)
        for k in range(links):
            back_terms += dot_nn(seps_ref[slot_of(links_ref[i, k], z)].astype(BF16), lower_ref[i * links + k])
        remainder = (forward_ref[i].astype(F32) - back_terms).astype(BF16)
        leaf_ref[i] = dot_nn(remainder, inverse_ref[i]).astype(BF16)


def stay(array):
    return pltpu.with_memory_space_constraint(array, pltpu.HBM)


def call(kernel, outs, in_specs, scratch=()):
    many = isinstance(outs, tuple)
    return pl.pallas_call(
        kernel,
        out_shape=outs,
        in_specs=in_specs,
        out_specs=tuple(VMEM for _ in outs) if many else VMEM,
        scratch_shapes=scratch,
        compiler_params=PARAMS,
    )


def shards(leaf_rhs, leaf_inverse, leaf_lower, leaf_links, sep_rhs, sep_inverse):
    leaves, links = leaf_links.shape
    shape = jax.ShapeDtypeStruct
    face = (NFACE, NSLOT * 2 * RP, LANES)
    column = (NZ, 2 * RP, LANES)
    lower = leaf_lower.reshape(leaves * links, B, B)
    forward, keep, send = call(
        link_kernel,
        (shape((leaves, R, B), BF16), shape(face, F32), shape(face, BF16)),
        [HBM, HBM, HBM, HBM],
        (
            pltpu.SMEM((leaves, links), jnp.int32),
            pltpu.VMEM((leaves, R, B), BF16),
            pltpu.VMEM((leaves, B, B), BF16),
            pltpu.VMEM((leaves * links, B, B), BF16),
            pltpu.VMEM((NY * NSLOT, R, B), F32),
            pltpu.SemaphoreType.DMA((CHUNKS + 3,)),
        ),
    )(*map(stay, (leaf_links, leaf_rhs, leaf_inverse, lower)))
    sent = lax.all_gather(send, "c")
    pairs = call(pair_kernel, shape(face, BF16), [VMEM, VMEM])(keep, sent)
    parts = lax.all_to_all(pairs, FACE, 0, 0, tiled=True)
    sums = call(face_kernel, shape(column, BF16), [VMEM])(parts)
    parts = lax.all_to_all(sums, "z", 0, 0, tiled=True)
    solved = call(
        solve_kernel, shape(column, BF16), [VMEM, VMEM, VMEM], (pltpu.VMEM((R, B), F32),)
    )(parts, sep_rhs, sep_inverse)
    planes = lax.all_to_all(solved, "z", 0, 0, tiled=True)
    picked = call(pick_kernel, shape(face, BF16), [VMEM])(planes)
    half = lax.all_to_all(picked, FACE, 0, 0, tiled=True)
    parts = lax.all_gather(half, "c")
    return call(
        back_kernel,
        (shape((leaves, R, B), BF16), shape((1, R, B), BF16)),
        [VMEM] * 5,
        (
            pltpu.SMEM((leaves, links), jnp.int32),
            pltpu.VMEM((NY * NSLOT, R, B), F32),
            pltpu.SemaphoreType.DMA(()),
        ),
    )(leaf_links, parts, lower, forward, leaf_inverse)


def solution(mesh):
    grid = Mesh(mesh.devices.reshape(NZ, NY, NX, NC), ("z", "y", "x", "c"))
    every, row = ("z", "y", "x", "c"), ("z", "y")
    return jax.shard_map(
        shards,
        mesh=grid,
        in_specs=(P(every), P(every), P(every), P(every), P(row), P(row)),
        out_specs=(P(every), P(row)),
        check_vma=False,
    )
```

```python
import jax
import jax.numpy as jnp
from jax import lax
from jax.experimental import pallas as pl
from jax.experimental.pallas import tpu as pltpu
from jax.sharding import Mesh
from jax.sharding import PartitionSpec as P

NZ, NY, NX, NC = 16, 4, 4, 2
FACE = ("y", "x")
NFACE = NY * NX
NEAR = (-2, -1, 0, 1, 2)
OWN, EDGE, FAR = 2, 5, 6
NSLOT = 7
R, B = 64, 256
RP = R // (NX * NC)
LANES = 128
CHUNKS = 3

F32, BF16 = jnp.float32, jnp.bfloat16
VMEM = pl.BlockSpec(memory_space=pltpu.VMEM)
SMEM = pl.BlockSpec(memory_space=pltpu.SMEM)
HBM = pl.BlockSpec(memory_space=pltpu.HBM)
PARAMS = pltpu.CompilerParams(vmem_limit_bytes=32 * 1024 * 1024)


def dot_nt(a, b):
    return lax.dot_general(a, b, (((1,), (1,)), ((), ())), preferred_element_type=F32)


def dot_nn(a, b):
    return lax.dot_general(a, b, (((1,), (0,)), ((), ())), preferred_element_type=F32)


def slot_of(link, z):
    step = (link // NY - z - NEAR[0] + NZ) % NZ
    plane_slot = jnp.where(step <= EDGE, step, jnp.where(step == NZ - 1, EDGE, FAR))
    return (link % NY) * NSLOT + plane_slot


def plane_of(step, z):
    return (z + step + NZ) % NZ


def rows_of(x, c):
    return pl.ds(pl.multiple_of((c * NX + x) * RP, RP), RP)


def fold(rows):
    return jnp.concatenate([rows[..., :LANES], rows[..., LANES:]], axis=-2)


def unfold(tile):
    return jnp.concatenate([tile[..., :RP, :], tile[..., RP:, :]], axis=-1)


def link_kernel(links_hbm, rhs_hbm, inverse_hbm, lower_hbm, forward_ref, keep_ref, send_ref, slots_ref,
                links_ref, rhs_ref, inverse_ref, lower_ref, terms_ref, sems):
    leaves, links = links_ref.shape
    per = leaves * links // CHUNKS
    copies = [
        pltpu.make_async_copy(links_hbm, links_ref, sems.at[CHUNKS]),
        pltpu.make_async_copy(rhs_hbm, rhs_ref, sems.at[CHUNKS + 1]),
        pltpu.make_async_copy(inverse_hbm, inverse_ref, sems.at[CHUNKS + 2]),
    ] + [
        pltpu.make_async_copy(lower_hbm.at[pl.ds(n * per, per)], lower_ref.at[pl.ds(n * per, per)], sems.at[n])
        for n in range(CHUNKS)
    ]
    for copy in copies:
        copy.start()
    small, blocks = copies[1:3], copies[3:]
    z, c = lax.axis_index("z"), lax.axis_index("c")
    terms_ref[...] = jnp.zeros_like(terms_ref)
    for copy in small:
        copy.wait()
    for i in range(leaves):
        forward_ref[i] = dot_nt(rhs_ref[i], inverse_ref[i]).astype(BF16)
    copies[0].wait()
    for i in range(leaves):
        forward = forward_ref[i]
        for k in range(links):
            n = i * links + k
            if n % per == 0:
                blocks[n // per].wait()
            slot = slot_of(links_ref[i, k], z)
            slots_ref[i, k] = slot
            terms_ref[slot] = dot_nt(forward, lower_ref[n])
    for y in range(NY):
        for x in range(NX):
            slots = slice(y * NSLOT, (y + 1) * NSLOT)
            mine = fold(terms_ref[slots, rows_of(x, c), :])
            keep_ref[y * NX + x] = mine.reshape(NSLOT * 2 * RP, LANES)
            other = fold(terms_ref[slots, rows_of(x, 1 - c), :])
            send_ref[y * NX + x] = other.reshape(NSLOT * 2 * RP, LANES).astype(BF16)


def pair_kernel(keep_ref, sent_ref, out_ref):
    out_ref[...] = (keep_ref[...] + sent_ref[1 - lax.axis_index("c")].astype(F32)).astype(BF16)


def face_kernel(parts_ref, out_ref):
    z, y = lax.axis_index("z"), lax.axis_index("y")
    rows = []
    for w in range(NY):
        total = parts_ref[w * NX].astype(F32)
        for x in range(1, NX):
            total = total + parts_ref[w * NX + x].astype(F32)
        rows.append(total.reshape(NSLOT, 2 * RP, LANES))
    total = rows[0] + rows[1] + rows[2] + rows[3]
    below = rows[0][EDGE]
    for w in range(1, NY):
        below = below + jnp.where(w <= y, rows[w][EDGE], 0.0)
    above = jnp.zeros_like(below)
    for w in range(1, NY):
        above = above + jnp.where(w > y, rows[w][EDGE], 0.0)
    out_ref[...] = jnp.zeros_like(out_ref)
    for slot, step in enumerate(NEAR):
        out_ref[plane_of(step, z)] = total[slot].astype(BF16)
    out_ref[plane_of(-3, z)] = below.astype(BF16)
    out_ref[plane_of(3, z)] = above.astype(BF16)
    out_ref[plane_of(NZ // 2, z)] = total[FAR].astype(BF16)


def solve_kernel(parts_ref, rhs_ref, inverse_ref, out_ref, rhs32_ref):
    rhs32_ref[...] = rhs_ref[0].astype(F32)
    sums = parts_ref[0].astype(F32)
    for n in range(1, NZ):
        sums = sums + parts_ref[n].astype(F32)
    right_side = (rhs32_ref[rows_of(lax.axis_index("x"), lax.axis_index("c")), :] - unfold(sums)).astype(BF16)
    middle = dot_nt(right_side, inverse_ref[0]).astype(BF16)
    solved = dot_nn(middle, inverse_ref[0])
    out_ref[...] = jnp.broadcast_to(fold(solved).astype(BF16)[None], out_ref.shape)


def pick_kernel(planes_ref, out_ref):
    z, y = lax.axis_index("z"), lax.axis_index("y")
    near = [planes_ref[plane_of(step, z)] for step in NEAR]
    below, above, far = (planes_ref[plane_of(step, z)] for step in (-3, 3, NZ // 2))
    for w in range(NY):
        edge = jnp.where(w <= y, below.astype(F32), above.astype(F32)).astype(BF16)
        picked = jnp.concatenate(near + [edge, far], axis=0)
        for x in range(NX):
            out_ref[w * NX + x] = picked


def back_kernel(slots_ref, parts_ref, lower_ref, forward_ref, inverse_ref, leaf_ref, sep_ref, seps_ref):
    leaves, links = slots_ref.shape
    y = lax.axis_index("y")
    for w in range(NY):
        for r in range(NC * NX):
            part = parts_ref[r // NX, w * NX + r % NX].astype(F32).reshape(NSLOT, 2 * RP, LANES)
            seps_ref[w * NSLOT:(w + 1) * NSLOT, r * RP:(r + 1) * RP, :] = unfold(part)
    sep_ref[0] = seps_ref[y * NSLOT + OWN].astype(BF16)
    remainders = []
    for i in range(leaves):
        back_terms = jnp.zeros((R, B), F32)
        for k in range(links):
            back_terms += dot_nn(seps_ref[slots_ref[i, k]].astype(BF16), lower_ref[i * links + k])
        remainders.append((forward_ref[i].astype(F32) - back_terms).astype(BF16))
    for i in range(leaves):
        leaf_ref[i] = dot_nn(remainders[i], inverse_ref[i]).astype(BF16)


def stay(array):
    return pltpu.with_memory_space_constraint(array, pltpu.HBM)


def call(kernel, outs, in_specs, scratch=(), out_specs=VMEM):
    return pl.pallas_call(
        kernel,
        out_shape=outs,
        in_specs=in_specs,
        out_specs=out_specs,
        scratch_shapes=scratch,
        compiler_params=PARAMS,
    )


def shards(leaf_rhs, leaf_inverse, leaf_lower, leaf_links, sep_rhs, sep_inverse):
    leaves, links = leaf_links.shape
    shape = jax.ShapeDtypeStruct
    face = (NFACE, NSLOT * 2 * RP, LANES)
    column = (NZ, 2 * RP, LANES)
    lower = leaf_lower.reshape(leaves * links, B, B)
    forward, keep, send, slots = call(
        link_kernel,
        (shape((leaves, R, B), BF16), shape(face, F32), shape(face, BF16), pltpu.SMEM((leaves, links), jnp.int32)),
        [HBM, HBM, HBM, HBM],
        (
            pltpu.SMEM((leaves, links), jnp.int32),
            pltpu.VMEM((leaves, R, B), BF16),
            pltpu.VMEM((leaves, B, B), BF16),
            pltpu.VMEM((leaves * links, B, B), BF16),
            pltpu.VMEM((NY * NSLOT, R, B), F32),
            pltpu.SemaphoreType.DMA((CHUNKS + 3,)),
        ),
        (VMEM, VMEM, VMEM, SMEM),
    )(*map(stay, (leaf_links, leaf_rhs, leaf_inverse, lower)))
    sent = lax.all_gather(send, "c")
    pairs = call(pair_kernel, shape(face, BF16), [VMEM, VMEM])(keep, sent)
    parts = lax.all_to_all(pairs, FACE, 0, 0, tiled=True)
    sums = call(face_kernel, shape(column, BF16), [VMEM])(parts)
    parts = lax.all_to_all(sums, "z", 0, 0, tiled=True)
    solved = call(
        solve_kernel, shape(column, BF16), [VMEM, VMEM, VMEM], (pltpu.VMEM((R, B), F32),)
    )(parts, sep_rhs, sep_inverse)
    planes = lax.all_to_all(solved, "z", 0, 0, tiled=True)
    picked = call(pick_kernel, shape(face, BF16), [VMEM])(planes)
    half = lax.all_to_all(picked, FACE, 0, 0, tiled=True)
    parts = lax.all_gather(half, "c")
    return call(
        back_kernel,
        (shape((leaves, R, B), BF16), shape((1, R, B), BF16)),
        [SMEM] + [VMEM] * 4,
        (pltpu.VMEM((NY * NSLOT, R, B), F32),),
        (VMEM, VMEM),
    )(slots, parts, lower, forward, leaf_inverse)


def solution(mesh):
    grid = Mesh(mesh.devices.reshape(NZ, NY, NX, NC), ("z", "y", "x", "c"))
    every, row = ("z", "y", "x", "c"), ("z", "y")
    return jax.shard_map(
        shards,
        mesh=grid,
        in_specs=(P(every), P(every), P(every), P(every), P(row), P(row)),
        out_specs=(P(every), P(row)),
        check_vma=False,
    )
```

```python
import jax
import jax.numpy as jnp
from jax import lax
from jax.experimental import pallas as pl
from jax.experimental.pallas import tpu as pltpu
from jax.sharding import Mesh
from jax.sharding import PartitionSpec as P

NZ, NY, NX, NC = 16, 4, 4, 2
FACE = ("y", "x")
NFACE = NY * NX
FIRST_PLANE, FIRST_PLACE = 8, 2 * NX + 2
PLANES = [[(FIRST_PLANE + n) % NZ for n in range(NZ)]]
PLACES = [[(FIRST_PLACE + n) % NFACE for n in range(NFACE)]]
NEAR = (-2, -1, 0, 1, 2)
OWN, EDGE, FAR = 2, 5, 6
NSLOT = 7
R, B = 64, 256
RP = R // (NX * NC)
LANES = 128
CHUNKS = 3

F32, BF16 = jnp.float32, jnp.bfloat16
VMEM = pl.BlockSpec(memory_space=pltpu.VMEM)
SMEM = pl.BlockSpec(memory_space=pltpu.SMEM)
HBM = pl.BlockSpec(memory_space=pltpu.HBM)
PARAMS = pltpu.CompilerParams(vmem_limit_bytes=32 * 1024 * 1024)


def dot_nt(a, b):
    return lax.dot_general(a, b, (((1,), (1,)), ((), ())), preferred_element_type=F32)


def dot_nn(a, b):
    return lax.dot_general(a, b, (((1,), (0,)), ((), ())), preferred_element_type=F32)


def slot_of(link, z):
    step = (link // NY - z - NEAR[0] + NZ) % NZ
    plane_slot = jnp.where(step <= EDGE, step, jnp.where(step == NZ - 1, EDGE, FAR))
    return (link % NY) * NSLOT + plane_slot


def plane_of(step, z):
    return (z + step + 2 * NZ - FIRST_PLANE) % NZ


def place_of(y, x):
    return (y * NX + x + NFACE - FIRST_PLACE) % NFACE


def rows_of(x, c):
    return pl.ds(pl.multiple_of((c * NX + x) * RP, RP), RP)


def fold(rows):
    return jnp.concatenate([rows[..., :LANES], rows[..., LANES:]], axis=-2)


def unfold(tile):
    return jnp.concatenate([tile[..., :RP, :], tile[..., RP:, :]], axis=-1)


def link_kernel(links_hbm, rhs_hbm, inverse_hbm, lower_hbm, forward_ref, keep_ref, send_ref, slots_ref,
                links_ref, rhs_ref, inverse_ref, lower_ref, terms_ref, sems):
    leaves, links = links_ref.shape
    per = leaves * links // CHUNKS
    copies = [
        pltpu.make_async_copy(links_hbm, links_ref, sems.at[CHUNKS]),
        pltpu.make_async_copy(rhs_hbm, rhs_ref, sems.at[CHUNKS + 1]),
        pltpu.make_async_copy(inverse_hbm, inverse_ref, sems.at[CHUNKS + 2]),
    ] + [
        pltpu.make_async_copy(lower_hbm.at[pl.ds(n * per, per)], lower_ref.at[pl.ds(n * per, per)], sems.at[n])
        for n in range(CHUNKS)
    ]
    for copy in copies:
        copy.start()
    small, blocks = copies[1:3], copies[3:]
    z, c = lax.axis_index("z"), lax.axis_index("c")
    terms_ref[...] = jnp.zeros_like(terms_ref)
    for copy in small:
        copy.wait()
    for i in range(leaves):
        forward_ref[i] = dot_nt(rhs_ref[i], inverse_ref[i]).astype(BF16)
    copies[0].wait()
    for i in range(leaves):
        forward = forward_ref[i]
        for k in range(links):
            n = i * links + k
            if n % per == 0:
                blocks[n // per].wait()
            slot = slot_of(links_ref[i, k], z)
            slots_ref[i, k] = slot
            terms_ref[slot] = dot_nt(forward, lower_ref[n])
    for y in range(NY):
        for x in range(NX):
            slots = slice(y * NSLOT, (y + 1) * NSLOT)
            mine = fold(terms_ref[slots, rows_of(x, c), :])
            keep_ref[place_of(y, x)] = mine.reshape(NSLOT * 2 * RP, LANES)
            other = fold(terms_ref[slots, rows_of(x, 1 - c), :])
            send_ref[place_of(y, x)] = other.reshape(NSLOT * 2 * RP, LANES).astype(BF16)


def pair_kernel(keep_ref, sent_ref, out_ref):
    out_ref[...] = (keep_ref[...] + sent_ref[1 - lax.axis_index("c")].astype(F32)).astype(BF16)


def face_kernel(parts_ref, out_ref):
    z, y = lax.axis_index("z"), lax.axis_index("y")
    rows = []
    for w in range(NY):
        total = parts_ref[place_of(w, 0)].astype(F32)
        for x in range(1, NX):
            total = total + parts_ref[place_of(w, x)].astype(F32)
        rows.append(total.reshape(NSLOT, 2 * RP, LANES))
    total = rows[0] + rows[1] + rows[2] + rows[3]
    below = rows[0][EDGE]
    for w in range(1, NY):
        below = below + jnp.where(w <= y, rows[w][EDGE], 0.0)
    above = jnp.zeros_like(below)
    for w in range(1, NY):
        above = above + jnp.where(w > y, rows[w][EDGE], 0.0)
    out_ref[...] = jnp.zeros_like(out_ref)
    for slot, step in enumerate(NEAR):
        out_ref[plane_of(step, z)] = total[slot].astype(BF16)
    out_ref[plane_of(-3, z)] = below.astype(BF16)
    out_ref[plane_of(3, z)] = above.astype(BF16)
    out_ref[plane_of(NZ // 2, z)] = total[FAR].astype(BF16)


def solve_kernel(parts_ref, rhs_ref, inverse_ref, out_ref, rhs32_ref):
    rhs32_ref[...] = rhs_ref[0].astype(F32)
    sums = parts_ref[0].astype(F32)
    for n in range(1, NZ):
        sums = sums + parts_ref[n].astype(F32)
    right_side = (rhs32_ref[rows_of(lax.axis_index("x"), lax.axis_index("c")), :] - unfold(sums)).astype(BF16)
    middle = dot_nt(right_side, inverse_ref[0]).astype(BF16)
    solved = dot_nn(middle, inverse_ref[0])
    out_ref[...] = jnp.broadcast_to(fold(solved).astype(BF16)[None], out_ref.shape)


def pick_kernel(planes_ref, out_ref):
    z, y = lax.axis_index("z"), lax.axis_index("y")
    near = [planes_ref[plane_of(step, z)] for step in NEAR]
    below, above, far = (planes_ref[plane_of(step, z)] for step in (-3, 3, NZ // 2))
    for w in range(NY):
        edge = jnp.where(w <= y, below.astype(F32), above.astype(F32)).astype(BF16)
        picked = jnp.concatenate(near + [edge, far], axis=0)
        for x in range(NX):
            out_ref[place_of(w, x)] = picked


def back_kernel(slots_ref, parts_ref, lower_ref, forward_ref, inverse_ref, leaf_ref, sep_ref, seps_ref):
    leaves, links = slots_ref.shape
    y = lax.axis_index("y")
    for w in range(NY):
        for r in range(NC * NX):
            part = parts_ref[r // NX, place_of(w, r % NX)].astype(F32).reshape(NSLOT, 2 * RP, LANES)
            seps_ref[w * NSLOT:(w + 1) * NSLOT, r * RP:(r + 1) * RP, :] = unfold(part)
    sep_ref[0] = seps_ref[y * NSLOT + OWN].astype(BF16)
    remainders = []
    for i in range(leaves):
        back_terms = jnp.zeros((R, B), F32)
        for k in range(links):
            back_terms += dot_nn(seps_ref[slots_ref[i, k]].astype(BF16), lower_ref[i * links + k])
        remainders.append((forward_ref[i].astype(F32) - back_terms).astype(BF16))
    for i in range(leaves):
        leaf_ref[i] = dot_nn(remainders[i], inverse_ref[i]).astype(BF16)


def stay(array):
    return pltpu.with_memory_space_constraint(array, pltpu.HBM)


def call(kernel, outs, in_specs, scratch=(), out_specs=VMEM):
    return pl.pallas_call(
        kernel,
        out_shape=outs,
        in_specs=in_specs,
        out_specs=out_specs,
        scratch_shapes=scratch,
        compiler_params=PARAMS,
    )


def exchange(blocks, axes, order):
    return lax.all_to_all(blocks, axes, 0, 0, tiled=True, axis_index_groups=order)


def shards(leaf_rhs, leaf_inverse, leaf_lower, leaf_links, sep_rhs, sep_inverse):
    leaves, links = leaf_links.shape
    shape = jax.ShapeDtypeStruct
    face = (NFACE, NSLOT * 2 * RP, LANES)
    column = (NZ, 2 * RP, LANES)
    lower = leaf_lower.reshape(leaves * links, B, B)
    forward, keep, send, slots = call(
        link_kernel,
        (shape((leaves, R, B), BF16), shape(face, F32), shape(face, BF16), pltpu.SMEM((leaves, links), jnp.int32)),
        [HBM, HBM, HBM, HBM],
        (
            pltpu.SMEM((leaves, links), jnp.int32),
            pltpu.VMEM((leaves, R, B), BF16),
            pltpu.VMEM((leaves, B, B), BF16),
            pltpu.VMEM((leaves * links, B, B), BF16),
            pltpu.VMEM((NY * NSLOT, R, B), F32),
            pltpu.SemaphoreType.DMA((CHUNKS + 3,)),
        ),
        (VMEM, VMEM, VMEM, SMEM),
    )(*map(stay, (leaf_links, leaf_rhs, leaf_inverse, lower)))
    sent = lax.all_gather(send, "c")
    pairs = call(pair_kernel, shape(face, BF16), [VMEM, VMEM])(keep, sent)
    parts = exchange(pairs, FACE, PLACES)
    sums = call(face_kernel, shape(column, BF16), [VMEM])(parts)
    parts = exchange(sums, "z", PLANES)
    solved = call(
        solve_kernel, shape(column, BF16), [VMEM, VMEM, VMEM], (pltpu.VMEM((R, B), F32),)
    )(parts, sep_rhs, sep_inverse)
    planes = exchange(solved, "z", PLANES)
    picked = call(pick_kernel, shape(face, BF16), [VMEM])(planes)
    half = exchange(picked, FACE, PLACES)
    parts = lax.all_gather(half, "c")
    return call(
        back_kernel,
        (shape((leaves, R, B), BF16), shape((1, R, B), BF16)),
        [SMEM] + [VMEM] * 4,
        (pltpu.VMEM((NY * NSLOT, R, B), F32),),
        (VMEM, VMEM),
    )(slots, parts, lower, forward, leaf_inverse)


def solution(mesh):
    grid = Mesh(mesh.devices.reshape(NZ, NY, NX, NC), ("z", "y", "x", "c"))
    every, row = ("z", "y", "x", "c"), ("z", "y")
    return jax.shard_map(
        shards,
        mesh=grid,
        in_specs=(P(every), P(every), P(every), P(every), P(row), P(row)),
        out_specs=(P(every), P(row)),
        check_vma=False,
    )
```

```python
import jax
import jax.numpy as jnp
from jax import lax
from jax.experimental import pallas as pl
from jax.experimental.pallas import tpu as pltpu
from jax.sharding import Mesh
from jax.sharding import PartitionSpec as P

NZ, NY, NX, NC = 16, 4, 4, 2
FACE = ("y", "x")
NFACE = NY * NX
FIRST_PLANES, FIRST_PLACES = (8, 8), (10, 10)
NEAR = (-2, -1, 0, 1, 2)
OWN, EDGE, FAR = 2, 5, 6
NSLOT = 7
R, B = 64, 256
RP = R // (NX * NC)
LANES = 128
CHUNKS = 2

F32, BF16 = jnp.float32, jnp.bfloat16
VMEM = pl.BlockSpec(memory_space=pltpu.VMEM)
SMEM = pl.BlockSpec(memory_space=pltpu.SMEM)
HBM = pl.BlockSpec(memory_space=pltpu.HBM)
PARAMS = pltpu.CompilerParams(vmem_limit_bytes=32 * 1024 * 1024)


def dot_nt(a, b):
    return lax.dot_general(a, b, (((1,), (1,)), ((), ())), preferred_element_type=F32)


def dot_nn(a, b):
    return lax.dot_general(a, b, (((1,), (0,)), ((), ())), preferred_element_type=F32)


def slot_of(link, z):
    step = (link // NY - z - NEAR[0] + NZ) % NZ
    plane_slot = jnp.where(step <= EDGE, step, jnp.where(step == NZ - 1, EDGE, FAR))
    return (link % NY) * NSLOT + plane_slot


def plane_of(step, z, turn):
    return (z + step + 2 * NZ - FIRST_PLANES[turn]) % NZ


def place_of(y, x, turn):
    return (y * NX + x + NFACE - FIRST_PLACES[turn]) % NFACE


def rows_of(x, c):
    return pl.ds(pl.multiple_of((c * NX + x) * RP, RP), RP)


def fold(rows):
    return jnp.concatenate([rows[..., :LANES], rows[..., LANES:]], axis=-2)


def unfold(tile):
    return jnp.concatenate([tile[..., :RP, :], tile[..., RP:, :]], axis=-1)


def link_kernel(links_hbm, rhs_hbm, inverse_hbm, lower_hbm, forward_ref, keep_ref, send_ref, slots_ref,
                links_ref, rhs_ref, inverse_ref, lower_ref, terms_ref, sems):
    leaves, links = links_ref.shape
    per = leaves * links // CHUNKS
    copies = [
        pltpu.make_async_copy(links_hbm, links_ref, sems.at[CHUNKS]),
        pltpu.make_async_copy(rhs_hbm, rhs_ref, sems.at[CHUNKS + 1]),
        pltpu.make_async_copy(inverse_hbm, inverse_ref, sems.at[CHUNKS + 2]),
    ] + [
        pltpu.make_async_copy(lower_hbm.at[pl.ds(n * per, per)], lower_ref.at[pl.ds(n * per, per)], sems.at[n])
        for n in range(CHUNKS)
    ]
    for copy in copies:
        copy.start()
    small, blocks = copies[1:3], copies[3:]
    z, c = lax.axis_index("z"), lax.axis_index("c")
    terms_ref[...] = jnp.zeros_like(terms_ref)
    for copy in small:
        copy.wait()
    for i in range(leaves):
        forward_ref[i] = dot_nt(rhs_ref[i], inverse_ref[i]).astype(BF16)
    copies[0].wait()
    for i in range(leaves):
        forward = forward_ref[i]
        for k in range(links):
            n = i * links + k
            if n % per == 0:
                blocks[n // per].wait()
            slot = slot_of(links_ref[i, k], z)
            slots_ref[i, k] = slot
            terms_ref[slot] = dot_nt(forward, lower_ref[n])
    for y in range(NY):
        for x in range(NX):
            slots = slice(y * NSLOT, (y + 1) * NSLOT)
            mine = fold(terms_ref[slots, rows_of(x, c), :])
            keep_ref[place_of(y, x, 0)] = mine.reshape(NSLOT * 2 * RP, LANES)
            other = fold(terms_ref[slots, rows_of(x, 1 - c), :])
            send_ref[place_of(y, x, 0)] = other.reshape(NSLOT * 2 * RP, LANES).astype(BF16)


def pair_kernel(keep_ref, sent_ref, out_ref):
    out_ref[...] = (keep_ref[...] + sent_ref[1 - lax.axis_index("c")].astype(F32)).astype(BF16)


def face_kernel(parts_ref, out_ref):
    z, y = lax.axis_index("z"), lax.axis_index("y")
    rows = []
    for w in range(NY):
        total = parts_ref[place_of(w, 0, 0)].astype(F32)
        for x in range(1, NX):
            total = total + parts_ref[place_of(w, x, 0)].astype(F32)
        rows.append(total.reshape(NSLOT, 2 * RP, LANES))
    total = rows[0] + rows[1] + rows[2] + rows[3]
    below = rows[0][EDGE]
    for w in range(1, NY):
        below = below + jnp.where(w <= y, rows[w][EDGE], 0.0)
    above = jnp.zeros_like(below)
    for w in range(1, NY):
        above = above + jnp.where(w > y, rows[w][EDGE], 0.0)
    out_ref[...] = jnp.zeros_like(out_ref)
    for slot, step in enumerate(NEAR):
        out_ref[plane_of(step, z, 0)] = total[slot].astype(BF16)
    out_ref[plane_of(-3, z, 0)] = below.astype(BF16)
    out_ref[plane_of(3, z, 0)] = above.astype(BF16)
    out_ref[plane_of(NZ // 2, z, 0)] = total[FAR].astype(BF16)


def solve_kernel(parts_ref, rhs_ref, inverse_ref, out_ref, rhs32_ref):
    rhs32_ref[...] = rhs_ref[0].astype(F32)
    sums = parts_ref[0].astype(F32)
    for n in range(1, NZ):
        sums = sums + parts_ref[n].astype(F32)
    right_side = (rhs32_ref[rows_of(lax.axis_index("x"), lax.axis_index("c")), :] - unfold(sums)).astype(BF16)
    middle = dot_nt(right_side, inverse_ref[0]).astype(BF16)
    solved = dot_nn(middle, inverse_ref[0])
    out_ref[...] = jnp.broadcast_to(fold(solved).astype(BF16)[None], out_ref.shape)


def pick_kernel(planes_ref, out_ref):
    z, y = lax.axis_index("z"), lax.axis_index("y")
    near = [planes_ref[plane_of(step, z, 1)] for step in NEAR]
    below, above, far = (planes_ref[plane_of(step, z, 1)] for step in (-3, 3, NZ // 2))
    for w in range(NY):
        edge = jnp.where(w <= y, below.astype(F32), above.astype(F32)).astype(BF16)
        picked = jnp.concatenate(near + [edge, far], axis=0)
        for x in range(NX):
            out_ref[place_of(w, x, 1)] = picked


def back_kernel(slots_ref, parts_ref, lower_ref, forward_ref, inverse_ref, leaf_ref, sep_ref, seps_ref):
    leaves, links = slots_ref.shape
    y = lax.axis_index("y")
    for w in range(NY):
        for r in range(0, NC * NX, 2):
            pair = [
                unfold(parts_ref[n // NX, place_of(w, n % NX, 1)].astype(F32).reshape(NSLOT, 2 * RP, LANES))
                for n in (r, r + 1)
            ]
            seps_ref[w * NSLOT:(w + 1) * NSLOT, r * RP:(r + 2) * RP, :] = jnp.concatenate(pair, axis=1).astype(BF16)
    sep_ref[0] = seps_ref[y * NSLOT + OWN]
    remainders = []
    for i in range(leaves):
        back_terms = jnp.zeros((R, B), F32)
        for k in range(links):
            back_terms += dot_nn(seps_ref[slots_ref[i, k]], lower_ref[i * links + k])
        remainders.append((forward_ref[i].astype(F32) - back_terms).astype(BF16))
    for i in range(leaves):
        leaf_ref[i] = dot_nn(remainders[i], inverse_ref[i]).astype(BF16)


def stay(array):
    return pltpu.with_memory_space_constraint(array, pltpu.HBM)


def call(kernel, outs, in_specs, scratch=(), out_specs=VMEM):
    return pl.pallas_call(
        kernel,
        out_shape=outs,
        in_specs=in_specs,
        out_specs=out_specs,
        scratch_shapes=scratch,
        compiler_params=PARAMS,
    )


def exchange(blocks, axes, first):
    count = blocks.shape[0]
    order = [[(first + n) % count for n in range(count)]]
    return lax.all_to_all(blocks, axes, 0, 0, tiled=True, axis_index_groups=order)


def shards(leaf_rhs, leaf_inverse, leaf_lower, leaf_links, sep_rhs, sep_inverse):
    leaves, links = leaf_links.shape
    shape = jax.ShapeDtypeStruct
    face = (NFACE, NSLOT * 2 * RP, LANES)
    column = (NZ, 2 * RP, LANES)
    lower = leaf_lower.reshape(leaves * links, B, B)
    forward, keep, send, slots = call(
        link_kernel,
        (shape((leaves, R, B), BF16), shape(face, F32), shape(face, BF16), pltpu.SMEM((leaves, links), jnp.int32)),
        [HBM, HBM, HBM, HBM],
        (
            pltpu.SMEM((leaves, links), jnp.int32),
            pltpu.VMEM((leaves, R, B), BF16),
            pltpu.VMEM((leaves, B, B), BF16),
            pltpu.VMEM((leaves * links, B, B), BF16),
            pltpu.VMEM((NY * NSLOT, R, B), F32),
            pltpu.SemaphoreType.DMA((CHUNKS + 3,)),
        ),
        (VMEM, VMEM, VMEM, SMEM),
    )(*map(stay, (leaf_links, leaf_rhs, leaf_inverse, lower)))
    sent = lax.all_gather(send, "c")
    pairs = call(pair_kernel, shape(face, BF16), [VMEM, VMEM])(keep, sent)
    parts = exchange(pairs, FACE, FIRST_PLACES[0])
    sums = call(face_kernel, shape(column, BF16), [VMEM])(parts)
    parts = exchange(sums, "z", FIRST_PLANES[0])
    solved = call(
        solve_kernel, shape(column, BF16), [VMEM, VMEM, VMEM], (pltpu.VMEM((R, B), F32),)
    )(parts, sep_rhs, sep_inverse)
    planes = exchange(solved, "z", FIRST_PLANES[1])
    picked = call(pick_kernel, shape(face, BF16), [VMEM])(planes)
    half = exchange(picked, FACE, FIRST_PLACES[1])
    parts = lax.all_gather(half, "c")
    return call(
        back_kernel,
        (shape((leaves, R, B), BF16), shape((1, R, B), BF16)),
        [SMEM] + [VMEM] * 4,
        (pltpu.VMEM((NY * NSLOT, R, B), BF16),),
        (VMEM, VMEM),
    )(slots, parts, lower, forward, leaf_inverse)


def solution(mesh):
    grid = Mesh(mesh.devices.reshape(NZ, NY, NX, NC), ("z", "y", "x", "c"))
    every, row = ("z", "y", "x", "c"), ("z", "y")
    return jax.shard_map(
        shards,
        mesh=grid,
        in_specs=(P(every), P(every), P(every), P(every), P(row), P(row)),
        out_specs=(P(every), P(row)),
        check_vma=False,
    )
```

```python
import jax
import jax.numpy as jnp
from jax import lax
from jax.experimental import pallas as pl
from jax.experimental.pallas import tpu as pltpu
from jax.sharding import Mesh
from jax.sharding import PartitionSpec as P

NZ, NY, NX, NC = 16, 4, 4, 2
FACE = ("y", "x")
NFACE = NY * NX
FIRST_PLANES, FIRST_PLACES = (8, 8), (10, 10)
NEAR = (-2, -1, 0, 1, 2)
OWN, EDGE, FAR = 2, 5, 6
NSLOT = 7
R, B = 64, 256
RP = R // (NX * NC)
LANES = 128
CHUNKS = 2

F32, BF16 = jnp.float32, jnp.bfloat16
VMEM = pl.BlockSpec(memory_space=pltpu.VMEM)
SMEM = pl.BlockSpec(memory_space=pltpu.SMEM)
HBM = pl.BlockSpec(memory_space=pltpu.HBM)
PARAMS = pltpu.CompilerParams(vmem_limit_bytes=32 * 1024 * 1024)


def dot_nt(a, b):
    return lax.dot_general(a, b, (((1,), (1,)), ((), ())), preferred_element_type=F32)


def dot_nn(a, b):
    return lax.dot_general(a, b, (((1,), (0,)), ((), ())), preferred_element_type=F32)


def slot_of(link, z):
    step = (link // NY - z - NEAR[0] + NZ) % NZ
    plane_slot = jnp.where(step <= EDGE, step, jnp.where(step == NZ - 1, EDGE, FAR))
    return (link % NY) * NSLOT + plane_slot


def plane_of(step, z, turn):
    return (z + step + 2 * NZ - FIRST_PLANES[turn]) % NZ


def place_of(y, x, turn):
    return (y * NX + x + NFACE - FIRST_PLACES[turn]) % NFACE


def rows_of(x, c):
    return pl.ds(pl.multiple_of((c * NX + x) * RP, RP), RP)


def fold(rows):
    return jnp.concatenate([rows[..., :LANES], rows[..., LANES:]], axis=-2)


def unfold(tile):
    return jnp.concatenate([tile[..., :RP, :], tile[..., RP:, :]], axis=-1)


def link_kernel(links_hbm, rhs_hbm, inverse_hbm, lower_hbm, forward_ref, keep_ref, send_ref, slots_ref,
                links_ref, rhs_ref, inverse_ref, lower_ref, terms_ref, sems):
    leaves, links = links_ref.shape
    per = leaves * links // CHUNKS
    copies = [
        pltpu.make_async_copy(links_hbm, links_ref, sems.at[CHUNKS]),
        pltpu.make_async_copy(rhs_hbm, rhs_ref, sems.at[CHUNKS + 1]),
        pltpu.make_async_copy(inverse_hbm, inverse_ref, sems.at[CHUNKS + 2]),
    ] + [
        pltpu.make_async_copy(lower_hbm.at[pl.ds(n * per, per)], lower_ref.at[pl.ds(n * per, per)], sems.at[n])
        for n in range(CHUNKS)
    ]
    for copy in copies:
        copy.start()
    small, blocks = copies[1:3], copies[3:]
    z, c = lax.axis_index("z"), lax.axis_index("c")
    terms_ref[...] = jnp.zeros_like(terms_ref)
    for copy in small:
        copy.wait()
    for i in range(leaves):
        forward_ref[i] = dot_nt(rhs_ref[i], inverse_ref[i]).astype(BF16)
    copies[0].wait()
    for i in range(leaves):
        forward = forward_ref[i]
        for k in range(links):
            n = i * links + k
            if n % per == 0:
                blocks[n // per].wait()
            slot = slot_of(links_ref[i, k], z)
            slots_ref[i, k] = slot
            terms_ref[slot] = dot_nt(forward, lower_ref[n])
    for y in range(NY):
        for x in range(NX):
            slots = slice(y * NSLOT, (y + 1) * NSLOT)
            mine = fold(terms_ref[slots, rows_of(x, c), :])
            keep_ref[place_of(y, x, 0)] = mine.reshape(NSLOT * 2 * RP, LANES)
            other = fold(terms_ref[slots, rows_of(x, 1 - c), :])
            send_ref[place_of(y, x, 0)] = other.reshape(NSLOT * 2 * RP, LANES).astype(BF16)


def pair_kernel(keep_ref, sent_ref, out_ref):
    out_ref[...] = (keep_ref[...] + sent_ref[1 - lax.axis_index("c")].astype(F32)).astype(BF16)


def face_kernel(parts_ref, out_ref):
    z, y = lax.axis_index("z"), lax.axis_index("y")
    rows = []
    for w in range(NY):
        total = parts_ref[place_of(w, 0, 0)].astype(F32)
        for x in range(1, NX):
            total = total + parts_ref[place_of(w, x, 0)].astype(F32)
        rows.append(total.reshape(NSLOT, 2 * RP, LANES))
    total = rows[0] + rows[1] + rows[2] + rows[3]
    below = rows[0][EDGE]
    for w in range(1, NY):
        below = below + jnp.where(w <= y, rows[w][EDGE], 0.0)
    above = jnp.zeros_like(below)
    for w in range(1, NY):
        above = above + jnp.where(w > y, rows[w][EDGE], 0.0)
    out_ref[...] = jnp.zeros_like(out_ref)
    for slot, step in enumerate(NEAR):
        out_ref[plane_of(step, z, 0)] = total[slot].astype(BF16)
    out_ref[plane_of(-3, z, 0)] = below.astype(BF16)
    out_ref[plane_of(3, z, 0)] = above.astype(BF16)
    out_ref[plane_of(NZ // 2, z, 0)] = total[FAR].astype(BF16)


def solve_kernel(parts_ref, rhs_ref, inverse_ref, out_ref, rhs32_ref):
    rhs32_ref[...] = rhs_ref[0].astype(F32)
    sums = [parts_ref[n].astype(F32) for n in range(NZ)]
    while len(sums) > 1:
        sums = [a + b for a, b in zip(sums[::2], sums[1::2], strict=True)]
    right_side = (rhs32_ref[rows_of(lax.axis_index("x"), lax.axis_index("c")), :] - unfold(sums[0])).astype(BF16)
    middle = dot_nt(right_side, inverse_ref[0]).astype(BF16)
    solved = dot_nn(middle, inverse_ref[0])
    out_ref[...] = jnp.broadcast_to(fold(solved).astype(BF16)[None], out_ref.shape)


def pick_kernel(planes_ref, out_ref):
    z, y = lax.axis_index("z"), lax.axis_index("y")
    near = [planes_ref[plane_of(step, z, 1)] for step in NEAR]
    below, above, far = (planes_ref[plane_of(step, z, 1)] for step in (-3, 3, NZ // 2))
    for w in range(NY):
        edge = jnp.where(w <= y, below.astype(F32), above.astype(F32)).astype(BF16)
        picked = jnp.concatenate(near + [edge, far], axis=0)
        for x in range(NX):
            out_ref[place_of(w, x, 1)] = picked


def back_kernel(slots_ref, parts_ref, lower_ref, forward_ref, inverse_ref, leaf_ref, sep_ref, seps_ref):
    leaves, links = slots_ref.shape
    y = lax.axis_index("y")
    for w in range(NY):
        for r in range(0, NC * NX, 2):
            pair = [
                unfold(parts_ref[n // NX, place_of(w, n % NX, 1)].astype(F32).reshape(NSLOT, 2 * RP, LANES))
                for n in (r, r + 1)
            ]
            seps_ref[w * NSLOT:(w + 1) * NSLOT, r * RP:(r + 2) * RP, :] = jnp.concatenate(pair, axis=1).astype(BF16)
    sep_ref[0] = seps_ref[y * NSLOT + OWN]
    remainders = []
    for i in range(leaves):
        back_terms = jnp.zeros((R, B), F32)
        for k in range(links):
            back_terms += dot_nn(seps_ref[slots_ref[i, k]], lower_ref[i * links + k])
        remainders.append((forward_ref[i].astype(F32) - back_terms).astype(BF16))
    for i in range(leaves):
        leaf_ref[i] = dot_nn(remainders[i], inverse_ref[i]).astype(BF16)


def stay(array):
    return pltpu.with_memory_space_constraint(array, pltpu.HBM)


def call(kernel, outs, in_specs, scratch=(), out_specs=VMEM):
    return pl.pallas_call(
        kernel,
        out_shape=outs,
        in_specs=in_specs,
        out_specs=out_specs,
        scratch_shapes=scratch,
        compiler_params=PARAMS,
    )


def exchange(blocks, axes, first):
    count = blocks.shape[0]
    order = [[(first + n) % count for n in range(count)]]
    return lax.all_to_all(blocks, axes, 0, 0, tiled=True, axis_index_groups=order)


def shards(leaf_rhs, leaf_inverse, leaf_lower, leaf_links, sep_rhs, sep_inverse):
    leaves, links = leaf_links.shape
    shape = jax.ShapeDtypeStruct
    face = (NFACE, NSLOT * 2 * RP, LANES)
    column = (NZ, 2 * RP, LANES)
    lower = leaf_lower.reshape(leaves * links, B, B)
    forward, keep, send, slots = call(
        link_kernel,
        (shape((leaves, R, B), BF16), shape(face, F32), shape(face, BF16), pltpu.SMEM((leaves, links), jnp.int32)),
        [HBM, HBM, HBM, HBM],
        (
            pltpu.SMEM((leaves, links), jnp.int32),
            pltpu.VMEM((leaves, R, B), BF16),
            pltpu.VMEM((leaves, B, B), BF16),
            pltpu.VMEM((leaves * links, B, B), BF16),
            pltpu.VMEM((NY * NSLOT, R, B), F32),
            pltpu.SemaphoreType.DMA((CHUNKS + 3,)),
        ),
        (VMEM, VMEM, VMEM, SMEM),
    )(*map(stay, (leaf_links, leaf_rhs, leaf_inverse, lower)))
    sent = lax.all_gather(send, "c")
    pairs = call(pair_kernel, shape(face, BF16), [VMEM, VMEM])(keep, sent)
    parts = exchange(pairs, FACE, FIRST_PLACES[0])
    sums = call(face_kernel, shape(column, BF16), [VMEM])(parts)
    parts = exchange(sums, "z", FIRST_PLANES[0])
    solved = call(
        solve_kernel, shape(column, BF16), [VMEM, VMEM, VMEM], (pltpu.VMEM((R, B), F32),)
    )(parts, sep_rhs, sep_inverse)
    planes = exchange(solved, "z", FIRST_PLANES[1])
    picked = call(pick_kernel, shape(face, BF16), [VMEM])(planes)
    half = exchange(picked, FACE, FIRST_PLACES[1])
    parts = lax.all_gather(half, "c")
    return call(
        back_kernel,
        (shape((leaves, R, B), BF16), shape((1, R, B), BF16)),
        [SMEM] + [VMEM] * 4,
        (pltpu.VMEM((NY * NSLOT, R, B), BF16),),
        (VMEM, VMEM),
    )(slots, parts, lower, forward, leaf_inverse)


def solution(mesh):
    grid = Mesh(mesh.devices.reshape(NZ, NY, NX, NC), ("z", "y", "x", "c"))
    every, row = ("z", "y", "x", "c"), ("z", "y")
    return jax.shard_map(
        shards,
        mesh=grid,
        in_specs=(P(every), P(every), P(every), P(every), P(row), P(row)),
        out_specs=(P(every), P(row)),
        check_vma=False,
    )
```
